32 devices in a mesh: job: 2 (over y), row: 4 (over z), slab: 2 (over x), pair: 2 (over core).
Axes of the slice: x: 2, y: 2, z: 4, core: 2. Of those that a mesh axis runs over, the one named last changes fastest.
Arguments:
- points: bfloat16 [32, 4096], P(None, ('job', 'row', 'slab', 'pair')), parts along dimension 1, may hold values from -5.2 to 5.2
- test_matrix: bfloat16 [256, 2048], P(None, ('row', 'slab', 'pair')), may hold values from -5 to 5
Outputs:
- sketch: float32 [4096, 256], P(('job', 'row', 'slab', 'pair')), parts along dimension 0
- core_matrix: float32 [512, 256], P('job'), parts along dimension 0
- upper_factor: float32 [512, 256], P('job'), parts along dimension 0
The draws below stay inside these ranges and needn't reach their ends.
There are 2 independent parts, one for each index of `job`. The reference program is written for one: setup_inputs(seed, part) draws one part's arguments, and reference() takes and returns one part's arrays. A program takes and returns all parts, laid end to end along the dimension named above; an argument that names none is the same for every part. Nothing has to cross between parts.
All inputs are finite; a program needn't handle non-finite values.
Results may differ from the reference program's by a relative error of at most 0.0026.
Values may be sent and summed in bfloat16 or wider, within the bound.
A program may use at most 64 MiB of HBM per device.

```python
import math
import jax
import jax.numpy as jnp
from jax import lax

F = 32
R = 256
ROWS_DEV = 128
POINTS = 2048
CLUSTERS = 128
N_SLAB = 2
N_PAIR = 2


def draw_points(key, part):
    centers = jax.random.truncated_normal(jax.random.fold_in(key, 1), -4.0, 4.0, (F, CLUSTERS), jnp.float32)
    assign = jax.random.randint(jax.random.fold_in(key, 2), (POINTS,), 0, CLUSTERS)
    jitter = 0.3 * jax.random.truncated_normal(jax.random.fold_in(key, 3), -4.0, 4.0, (F, POINTS), jnp.float32)
    values = jnp.take(centers, assign, axis=1) + jitter
    return values.astype(jnp.bfloat16)


def shard_levels(rng, dims, pieces, smallest, top_value):
    level, own = 1.0, jax.random.fold_in(rng, 6)
    for dim, blocks in pieces:
        draws = jnp.exp(jax.random.uniform(jax.random.fold_in(own, dim), (blocks,), jnp.float32, smallest / len(pieces), top_value / len(pieces)))
        level = level * jnp.repeat(draws, dims[dim] // blocks).reshape([-1 if axis == dim else 1 for axis in range(len(dims))])
    return level


def normal_values(stream_key, extent, spread, bound, shards=(), kind=jnp.bfloat16):
    entries = jax.random.normal(stream_key, extent, jnp.float32) * spread
    if len(shards) > 0:
        entries = shard_levels(stream_key, extent, shards, -0.22, 0.18) * entries
    return jnp.clip(entries, min=-bound, max=bound).astype(kind)


def setup_inputs(seed: int = 0, part: int = 0) -> dict:
    key_list = jax.random.split(jax.random.key(seed), 3)
    part_splits = jax.random.split(jax.random.fold_in(key_list[2], part), 3)
    return {
        "points": draw_points(jax.random.fold_in(jax.random.fold_in(key_list[2], part), 71), part),
        "test_matrix": normal_values(key_list[1], (R, POINTS), 1.0, 5.0, ((1, 16),)),
    }


def matern_tile(row_points, col_points, length_scale):
    row_squares = lax.optimization_barrier(jnp.sum(row_points.astype(jnp.float32) ** 2, axis=0))
    col_squares = lax.optimization_barrier(jnp.sum(col_points.astype(jnp.float32) ** 2, axis=0))
    inner = jnp.dot(row_points.T.astype(jnp.float32), col_points.astype(jnp.float32), preferred_element_type=jnp.float32)
    dist_sq = jnp.maximum(row_squares[:, None] + col_squares[None, :] - 2.0 * inner, 0.0)
    scaled = jnp.sqrt(dist_sq) / length_scale
    root_five = math.sqrt(5.0)
    values = (1.0 + root_five * scaled + 5.0 / 3.0 * scaled * scaled) * jnp.exp(-root_five * scaled)
    return values.astype(jnp.bfloat16)

def reference(points, test_matrix):
    length_scale = 0.35 * math.sqrt(F)
    block_size = ROWS_DEV * N_SLAB * N_PAIR
    blocks = POINTS // block_size
    stacked = points.reshape(F, blocks, block_size).transpose(1, 0, 2)

    def one_block(block_points):
        kernel_tile = matern_tile(block_points, points, length_scale)
        return lax.dot_general(kernel_tile.astype(jnp.float32), test_matrix.astype(jnp.float32), (((1,), (1,)), ((), ())), preferred_element_type=jnp.float32)
    sketch = lax.map(one_block, stacked).reshape(POINTS, R)
    gram = jnp.dot(sketch.T, sketch, precision=lax.Precision.HIGHEST) / POINTS
    core_matrix = jnp.dot(test_matrix.astype(jnp.float32), sketch, precision=lax.Precision.HIGHEST) / POINTS
    upper_factor = jnp.linalg.cholesky(gram).T
    return (sketch, core_matrix, upper_factor)
```

```python
import functools
import math

import jax
import jax.numpy as jnp
from jax import lax
from jax.experimental import pallas as pl
from jax.experimental.pallas import tpu as pltpu
from jax.sharding import PartitionSpec as P

MESH = pl.DeviceIdType.MESH


def loop(start, stop, body):
    if stop - start <= 8:
        for step in range(start, stop):
            body(step)
    else:
        lax.fori_loop(start, stop, lambda step, _: (body(step), 0)[1], 0)


def sketch_kernel(
    rows, slabs, pairs, points_ref, tests_ref, sketch_ref, core_ref, gram_ref,
    row_points, col_points, col_tests, part_out, part_in, plane, own_plane,
    terms, term_in, total,
    pt_sems, tt_sems, rp_sems, part_sems, plane_sems, term_sems, total_sems,
):
    block = slabs * pairs
    me_row = lax.axis_index("row")
    me = lax.axis_index("slab") * pairs + lax.axis_index("pair")
    feats, width = points_ref.shape
    tests = tests_ref.shape[0]
    chunk = tests // block

    def at_row(d):
        return lax.rem(me_row + d, rows)

    def at_block(d):
        return lax.rem(me + d, block)

    def block_id(index):
        return {"slab": index // pairs, "pair": lax.rem(index, pairs)}

    def lanes(index):
        return pl.ds(pl.multiple_of(index * width, width), width)

    def copy(src, dst, sems, to, sender, target):
        return pltpu.make_async_remote_copy(
            src_ref=src, dst_ref=dst, send_sem=sems.at[0, to], recv_sem=sems.at[1, sender],
            device_id=target, device_id_type=MESH,
        )

    barrier = pltpu.get_barrier_semaphore()
    loop(1, rows, lambda d: pl.semaphore_signal(
        barrier, inc=1, device_id={"row": at_row(d)}, device_id_type=MESH))
    loop(1, block, lambda d: pl.semaphore_signal(
        barrier, inc=1, device_id=block_id(at_block(d)), device_id_type=MESH))
    pl.semaphore_wait(barrier, rows + block - 2)

    def points_copy(to, sender):
        return copy(points_ref, col_points.at[:, lanes(sender)], pt_sems, to, sender, block_id(to))

    def tests_copy(to, sender):
        return copy(tests_ref, col_tests.at[:, lanes(sender)], tt_sems, to, sender, block_id(to))

    def row_copy(to, sender):
        return copy(points_ref, row_points.at[sender], rp_sems, to, sender, {"row": to})

    def part_copy(to, sender):
        return copy(part_out.at[to], part_in.at[sender], part_sems, to, sender, {"row": to})

    def plane_copy(to, sender):
        return copy(own_plane, plane.at[pl.ds(pl.multiple_of(sender * width, width), width), :],
                    plane_sems, to, sender, block_id(to))

    def term_copy(which, to, sender):
        return copy(terms.at[which, pl.ds(pl.multiple_of(me * chunk, chunk), chunk), :],
                    term_in.at[which, sender], term_sems.at[which], to, sender, {"row": to})

    def total_copy(which, to, sender):
        piece = pl.ds(pl.multiple_of(sender * chunk, chunk), chunk)
        return copy(total.at[which, piece, :], total.at[which, piece, :],
                    total_sems.at[which], to, sender, block_id(to))

    loop(1, block, lambda d: points_copy(at_block(d), me).start())
    loop(1, rows, lambda d: row_copy(at_row(d), me_row).start())
    loop(1, block, lambda d: tests_copy(at_block(d), me).start())
    row_points[me_row] = points_ref[...]
    col_points[:, lanes(me)] = points_ref[...]
    col_tests[:, lanes(me)] = tests_ref[...]

    length_scale = 0.35 * math.sqrt(feats)
    scale = 5.0 / (length_scale * length_scale)
    loop(1, block, lambda d: points_copy(at_block(d), at_block(d)).wait_recv())
    cols = col_points[...]
    cols32 = cols.astype(jnp.float32)
    col_squares = jnp.sum(cols32 * cols32, axis=0, keepdims=True) * scale

    def partial_sketch(row):
        picked = row_points[row].astype(jnp.float32).T
        squares = jnp.sum(picked * picked, axis=1, keepdims=True) * scale
        inner = jnp.dot(picked.astype(jnp.bfloat16), cols, preferred_element_type=jnp.float32)
        squared = jnp.maximum(squares + col_squares - (2.0 * scale) * inner, 1e-30)
        t = squared * lax.rsqrt(squared)
        tile = ((1.0 + t + squared * (1.0 / 3.0)) * jnp.exp(-t)).astype(jnp.bfloat16)
        return lax.dot_general(tile, col_tests[...], (((1,), (1,)), ((), ())),
                               preferred_element_type=jnp.float32)

    loop(1, block, lambda d: tests_copy(at_block(d), at_block(d)).wait_recv())

    def row_step(d):
        to = at_row(d)
        row_copy(to, to).wait_recv()
        part_out[to] = partial_sketch(to).astype(jnp.bfloat16)
        part_copy(to, me_row).start()

    loop(1, rows, row_step)
    sketch_ref[...] = partial_sketch(me_row)

    def part_step(d):
        part_copy(at_row(d), at_row(d)).wait_recv()
        sketch_ref[...] += part_in[at_row(d)].astype(jnp.float32)

    loop(1, rows, part_step)

    rounded = sketch_ref[...].astype(jnp.bfloat16)
    own_plane[...] = rounded
    loop(1, block, lambda d: plane_copy(at_block(d), me).start())
    plane[pl.ds(pl.multiple_of(me * width, width), width), :] = rounded
    loop(1, block, lambda d: plane_copy(at_block(d), at_block(d)).wait_recv())
    whole = plane[...]
    terms[0] = lax.dot_general(whole, whole, (((0,), (0,)), ((), ())),
                               preferred_element_type=jnp.float32)
    loop(1, rows, lambda d: term_copy(0, at_row(d), me_row).start())
    terms[1] = jnp.dot(col_tests[...], whole, preferred_element_type=jnp.float32)
    loop(1, rows, lambda d: term_copy(1, at_row(d), me_row).start())

    mine = pl.ds(pl.multiple_of(me * chunk, chunk), chunk)
    inverse = 1.0 / (width * rows * block)
    for which in (0, 1):
        term_in[which, me_row] = terms[which, mine, :]
        loop(1, rows, lambda d: term_copy(which, at_row(d), at_row(d)).wait_recv())
        total[which, mine, :] = jnp.sum(term_in[which], axis=0) * inverse
        loop(1, block, lambda d: total_copy(which, at_block(d), me).start())
    for which, out in ((0, gram_ref), (1, core_ref)):
        loop(1, block, lambda d: total_copy(which, at_block(d), at_block(d)).wait_recv())
        out[...] = total[which]

    def block_sent(d):
        to = at_block(d)
        for sent in (points_copy, tests_copy, plane_copy):
            sent(to, me).wait_send()
        for which in (0, 1):
            total_copy(which, to, me).wait_send()

    def row_sent(d):
        to = at_row(d)
        row_copy(to, me_row).wait_send()
        part_copy(to, me_row).wait_send()
        for which in (0, 1):
            term_copy(which, to, me_row).wait_send()

    loop(1, block, block_sent)
    loop(1, rows, row_sent)


def local(sizes, points, test_matrix):
    rows, slabs, pairs = sizes
    block = slabs * pairs
    feats, width = points.shape
    tests = test_matrix.shape[0]
    vmem = pl.BlockSpec(memory_space=pltpu.VMEM)
    square = jax.ShapeDtypeStruct((tests, tests), jnp.float32)
    sketch, core_matrix, gram = pl.pallas_call(
        functools.partial(sketch_kernel, rows, slabs, pairs),
        out_shape=(jax.ShapeDtypeStruct((width, tests), jnp.float32), square, square),
        in_specs=[vmem, vmem],
        out_specs=(vmem, vmem, vmem),
        scratch_shapes=[
            pltpu.VMEM((rows, feats, width), jnp.bfloat16),
            pltpu.VMEM((feats, block * width), jnp.bfloat16),
            pltpu.VMEM((tests, block * width), jnp.bfloat16),
            pltpu.VMEM((rows, width, tests), jnp.bfloat16),
            pltpu.VMEM((rows, width, tests), jnp.bfloat16),
            pltpu.VMEM((block * width, tests), jnp.bfloat16),
            pltpu.VMEM((width, tests), jnp.bfloat16),
            pltpu.VMEM((2, tests, tests), jnp.float32),
            pltpu.VMEM((2, rows, tests // block, tests), jnp.float32),
            pltpu.VMEM((2, tests, tests), jnp.float32),
            pltpu.SemaphoreType.DMA((2, block)),
            pltpu.SemaphoreType.DMA((2, block)),
            pltpu.SemaphoreType.DMA((2, rows)),
            pltpu.SemaphoreType.DMA((2, rows)),
            pltpu.SemaphoreType.DMA((2, block)),
            pltpu.SemaphoreType.DMA((2, 2, rows)),
            pltpu.SemaphoreType.DMA((2, 2, block)),
        ],
        compiler_params=pltpu.CompilerParams(
            collective_id=0, has_side_effects=True, vmem_limit_bytes=40 * 1024 * 1024
        ),
        name="sketch",
    )(points, test_matrix)
    upper_factor = jnp.linalg.cholesky(gram).T
    return (sketch, core_matrix, upper_factor)


def solution(mesh):
    sizes = tuple(mesh.shape[axis] for axis in ("row", "slab", "pair"))
    return jax.shard_map(
        functools.partial(local, sizes),
        mesh=mesh,
        in_specs=(P(None, ("job", "row", "slab", "pair")), P(None, ("row", "slab", "pair"))),
        out_specs=(P(("job", "row", "slab", "pair"), None), P("job", None), P("job", None)),
        check_vma=False,
    )
```

```python
import functools
import math

import jax
import jax.numpy as jnp
from jax import lax
from jax.experimental import pallas as pl
from jax.experimental.pallas import tpu as pltpu
from jax.sharding import PartitionSpec as P

MESH = pl.DeviceIdType.MESH


def loop(start, stop, body):
    if stop - start <= 8:
        for step in range(start, stop):
            body(step)
    else:
        lax.fori_loop(start, stop, lambda step, _: (body(step), 0)[1], 0)


def sketch_kernel(
    rows, slabs, pairs, points_ref, tests_ref, sketch_ref, core_ref, gram_ref,
    row_points, col_points, col_tests, part_out, part_in, plane, own_plane,
    terms, term_in, total,
    pt_sems, tt_sems, rp_sems, part_sems, plane_sems, term_sems, total_sems,
):
    block = slabs * pairs
    me_row = lax.axis_index("row")
    me = lax.axis_index("slab") * pairs + lax.axis_index("pair")
    feats, width = points_ref.shape
    tests = tests_ref.shape[0]
    chunk = tests // block

    def at_row(d):
        return lax.rem(me_row + d, rows)

    def at_block(d):
        return lax.rem(me + d, block)

    def block_id(index):
        return {"slab": index // pairs, "pair": lax.rem(index, pairs)}

    def lanes(index):
        return pl.ds(pl.multiple_of(index * width, width), width)

    def copy(src, dst, sems, to, sender, target):
        return pltpu.make_async_remote_copy(
            src_ref=src, dst_ref=dst, send_sem=sems.at[0, to], recv_sem=sems.at[1, sender],
            device_id=target, device_id_type=MESH,
        )

    barrier = pltpu.get_barrier_semaphore()
    loop(1, rows, lambda d: pl.semaphore_signal(
        barrier, inc=1, device_id={"row": at_row(d)}, device_id_type=MESH))
    loop(1, block, lambda d: pl.semaphore_signal(
        barrier, inc=1, device_id=block_id(at_block(d)), device_id_type=MESH))
    pl.semaphore_wait(barrier, rows + block - 2)

    def points_copy(to, sender):
        return copy(points_ref, col_points.at[:, lanes(sender)], pt_sems, to, sender, block_id(to))

    def tests_copy(to, sender):
        return copy(tests_ref, col_tests.at[:, lanes(sender)], tt_sems, to, sender, block_id(to))

    def row_copy(to, sender):
        return copy(points_ref, row_points.at[sender], rp_sems, to, sender, {"row": to})

    def part_copy(to, sender):
        return copy(part_out.at[to], part_in.at[sender], part_sems, to, sender, {"row": to})

    def plane_copy(to, sender):
        return copy(own_plane, plane.at[pl.ds(pl.multiple_of(sender * width, width), width), :],
                    plane_sems, to, sender, block_id(to))

    def term_copy(which, to, sender):
        return copy(terms.at[which, pl.ds(pl.multiple_of(me * chunk, chunk), chunk), :],
                    term_in.at[which, sender], term_sems.at[which], to, sender, {"row": to})

    def total_copy(which, to, sender):
        piece = pl.ds(pl.multiple_of(sender * chunk, chunk), chunk)
        return copy(total.at[which, piece, :], total.at[which, piece, :],
                    total_sems.at[which], to, sender, block_id(to))

    loop(1, block, lambda d: points_copy(at_block(d), me).start())
    loop(1, rows, lambda d: row_copy(at_row(d), me_row).start())
    loop(1, block, lambda d: tests_copy(at_block(d), me).start())
    row_points[me_row] = points_ref[...]
    col_points[:, lanes(me)] = points_ref[...]
    col_tests[:, lanes(me)] = tests_ref[...]

    length_scale = 0.35 * math.sqrt(feats)
    scale = 5.0 / (length_scale * length_scale)
    loop(1, block, lambda d: points_copy(at_block(d), at_block(d)).wait_recv())
    cols = col_points[...]
    cols32 = cols.astype(jnp.float32)
    col_squares = jnp.sum(cols32 * cols32, axis=0, keepdims=True) * scale

    def partial_sketch(row):
        picked = row_points[row].astype(jnp.float32).T
        squares = jnp.sum(picked * picked, axis=1, keepdims=True) * scale
        inner = jnp.dot(picked.astype(jnp.bfloat16), cols, preferred_element_type=jnp.float32)
        squared = jnp.maximum(squares + col_squares - (2.0 * scale) * inner, 1e-30)
        t = squared * lax.rsqrt(squared)
        tile = ((1.0 + t + squared * (1.0 / 3.0)) * jnp.exp(-t)).astype(jnp.bfloat16)
        return lax.dot_general(tile, col_tests[...], (((1,), (1,)), ((), ())),
                               preferred_element_type=jnp.float32)

    loop(1, block, lambda d: tests_copy(at_block(d), at_block(d)).wait_recv())

    def row_step(d):
        to = at_row(d)
        row_copy(to, to).wait_recv()
        part_out[to] = partial_sketch(to).astype(jnp.bfloat16)
        part_copy(to, me_row).start()

    loop(1, rows, row_step)
    sketch_ref[...] = partial_sketch(me_row)

    def part_step(d):
        part_copy(at_row(d), at_row(d)).wait_recv()
        sketch_ref[...] += part_in[at_row(d)].astype(jnp.float32)

    loop(1, rows, part_step)

    rounded = sketch_ref[...].astype(jnp.bfloat16)
    own_plane[...] = rounded
    loop(1, block, lambda d: plane_copy(at_block(d), me).start())
    plane[pl.ds(pl.multiple_of(me * width, width), width), :] = rounded
    loop(1, block, lambda d: plane_copy(at_block(d), at_block(d)).wait_recv())
    whole = plane[...]
    terms[0] = lax.dot_general(whole, whole, (((0,), (0,)), ((), ())),
                               preferred_element_type=jnp.float32)
    loop(1, rows, lambda d: term_copy(0, at_row(d), me_row).start())
    terms[1] = jnp.dot(col_tests[...], whole, preferred_element_type=jnp.float32)
    loop(1, rows, lambda d: term_copy(1, at_row(d), me_row).start())

    mine = pl.ds(pl.multiple_of(me * chunk, chunk), chunk)
    inverse = 1.0 / (width * rows * block)
    for which in (0, 1):
        term_in[which, me_row] = terms[which, mine, :]
        loop(1, rows, lambda d: term_copy(which, at_row(d), at_row(d)).wait_recv())
        total[which, mine, :] = jnp.sum(term_in[which], axis=0) * inverse
        loop(1, block, lambda d: total_copy(which, at_block(d), me).start())
    for which, out in ((0, gram_ref), (1, core_ref)):
        loop(1, block, lambda d: total_copy(which, at_block(d), at_block(d)).wait_recv())
        out[...] = total[which]

    def block_sent(d):
        to = at_block(d)
        for sent in (points_copy, tests_copy, plane_copy):
            sent(to, me).wait_send()
        for which in (0, 1):
            total_copy(which, to, me).wait_send()

    def row_sent(d):
        to = at_row(d)
        row_copy(to, me_row).wait_send()
        part_copy(to, me_row).wait_send()
        for which in (0, 1):
            term_copy(which, to, me_row).wait_send()

    loop(1, block, block_sent)
    loop(1, rows, row_sent)


def factor_kernel(gram_ref, upper_ref):
    size = gram_ref.shape[0]
    per, lanes = 8, 128
    wide = size // lanes
    group = lanes // per
    panels = [
        [gram_ref[q * per:(q + 1) * per, b * lanes:(b + 1) * lanes] for b in range(q // group, wide)]
        for q in range(size // per)
    ]
    row_id = lax.broadcasted_iota(jnp.int32, (per, lanes), 0)
    lane_id = lax.broadcasted_iota(jnp.int32, (per, lanes), 1)
    for p in range(size // per):
        first = p // group
        lane = p * per - first * lanes
        panel = panels[p]
        columns = [jnp.broadcast_to(panel[0][:, lane + j:lane + j + 1], (per, lanes)) for j in range(per)]
        small = [[columns[j][i:i + 1, :] for j in range(per)] for i in range(per)]
        rows = [[piece[i:i + 1, :] for piece in panel] for i in range(per)]
        for i in range(per):
            inverse = lax.rsqrt(small[i][i])
            for j in range(i + 1, per):
                small[i][j] = small[i][j] * inverse
            rows[i] = [piece * inverse for piece in rows[i]]
            for j in range(i + 1, per):
                for l in range(j, per):
                    small[j][l] = small[j][l] - small[i][j] * small[i][l]
                rows[j] = [a - small[i][j] * b for a, b in zip(rows[j], rows[i])]
        done = [jnp.concatenate([rows[i][b] for i in range(per)], axis=0) for b in range(wide - first)]
        done[0] = jnp.where(lane_id >= row_id + lane, done[0], 0.0)
        for b in range(wide):
            upper_ref[p * per:(p + 1) * per, b * lanes:(b + 1) * lanes] = (
                done[b - first] if b >= first else jnp.zeros((per, lanes), jnp.float32))
        turned = [piece.T for piece in done]
        for q in range(p + 1, size // per):
            start = q // group
            offset = q * per - start * lanes
            factors = turned[start - first][offset:offset + per, :]
            for i in range(per):
                factor = jnp.broadcast_to(factors[:, i:i + 1], (per, lanes))
                panels[q] = [
                    piece - factor * rows[i][start + b - first]
                    for b, piece in enumerate(panels[q])
                ]


def local(sizes, points, test_matrix):
    rows, slabs, pairs = sizes
    block = slabs * pairs
    feats, width = points.shape
    tests = test_matrix.shape[0]
    vmem = pl.BlockSpec(memory_space=pltpu.VMEM)
    square = jax.ShapeDtypeStruct((tests, tests), jnp.float32)
    sketch, core_matrix, gram = pl.pallas_call(
        functools.partial(sketch_kernel, rows, slabs, pairs),
        out_shape=(jax.ShapeDtypeStruct((width, tests), jnp.float32), square, square),
        in_specs=[vmem, vmem],
        out_specs=(vmem, vmem, vmem),
        scratch_shapes=[
            pltpu.VMEM((rows, feats, width), jnp.bfloat16),
            pltpu.VMEM((feats, block * width), jnp.bfloat16),
            pltpu.VMEM((tests, block * width), jnp.bfloat16),
            pltpu.VMEM((rows, width, tests), jnp.bfloat16),
            pltpu.VMEM((rows, width, tests), jnp.bfloat16),
            pltpu.VMEM((block * width, tests), jnp.bfloat16),
            pltpu.VMEM((width, tests), jnp.bfloat16),
            pltpu.VMEM((2, tests, tests), jnp.float32),
            pltpu.VMEM((2, rows, tests // block, tests), jnp.float32),
            pltpu.VMEM((2, tests, tests), jnp.float32),
            pltpu.SemaphoreType.DMA((2, block)),
            pltpu.SemaphoreType.DMA((2, block)),
            pltpu.SemaphoreType.DMA((2, rows)),
            pltpu.SemaphoreType.DMA((2, rows)),
            pltpu.SemaphoreType.DMA((2, block)),
            pltpu.SemaphoreType.DMA((2, 2, rows)),
            pltpu.SemaphoreType.DMA((2, 2, block)),
        ],
        compiler_params=pltpu.CompilerParams(
            collective_id=0, has_side_effects=True, vmem_limit_bytes=40 * 1024 * 1024
        ),
        name="sketch",
    )(points, test_matrix)
    upper_factor = pl.pallas_call(
        factor_kernel, out_shape=square, in_specs=[vmem], out_specs=vmem,
        compiler_params=pltpu.CompilerParams(vmem_limit_bytes=40 * 1024 * 1024),
        name="factor",
    )(gram)
    return (sketch, core_matrix, upper_factor)


def solution(mesh):
    sizes = tuple(mesh.shape[axis] for axis in ("row", "slab", "pair"))
    return jax.shard_map(
        functools.partial(local, sizes),
        mesh=mesh,
        in_specs=(P(None, ("job", "row", "slab", "pair")), P(None, ("row", "slab", "pair"))),
        out_specs=(P(("job", "row", "slab", "pair"), None), P("job", None), P("job", None)),
        check_vma=False,
    )
```

```python
import functools
import math

import jax
import jax.numpy as jnp
from jax import lax
from jax.experimental import pallas as pl
from jax.experimental.pallas import tpu as pltpu
from jax.sharding import PartitionSpec as P

MESH = pl.DeviceIdType.MESH


def loop(start, stop, body):
    if stop - start <= 8:
        for step in range(start, stop):
            body(step)
    else:
        lax.fori_loop(start, stop, lambda step, _: (body(step), 0)[1], 0)


def factor(blocks, size, upper_ref, halfway):
    per, lanes = 8, 128
    wide = size // lanes
    group = lanes // per
    panels = [
        [blocks[q // group, b][q % group * per:(q % group + 1) * per, :] for b in range(q // group, wide)]
        for q in range(size // per)
    ]
    row_id = lax.broadcasted_iota(jnp.int32, (per, lanes), 0)
    lane_id = lax.broadcasted_iota(jnp.int32, (per, lanes), 1)
    for p in range(size // per):
        if p == size // per // 2:
            halfway()
        first = p // group
        lane = p * per - first * lanes
        panel = panels[p]
        columns = [jnp.broadcast_to(panel[0][:, lane + j:lane + j + 1], (per, lanes)) for j in range(per)]
        small = [[columns[j][i:i + 1, :] for j in range(per)] for i in range(per)]
        rows = [[piece[i:i + 1, :] for piece in panel] for i in range(per)]
        for i in range(per):
            inverse = lax.rsqrt(small[i][i])
            for j in range(i + 1, per):
                small[i][j] = small[i][j] * inverse
            rows[i] = [piece * inverse for piece in rows[i]]
            for j in range(i + 1, per):
                for l in range(j, per):
                    small[j][l] = small[j][l] - small[i][j] * small[i][l]
                rows[j] = [a - small[i][j] * b for a, b in zip(rows[j], rows[i])]
        done = [jnp.concatenate([rows[i][b] for i in range(per)], axis=0) for b in range(wide - first)]
        done[0] = jnp.where(lane_id >= row_id + lane, done[0], 0.0)
        for b in range(wide):
            upper_ref[p * per:(p + 1) * per, b * lanes:(b + 1) * lanes] = (
                done[b - first] if b >= first else jnp.zeros((per, lanes), jnp.float32))
        turned = [piece.T for piece in done]
        for q in range(p + 1, size // per):
            start = q // group
            offset = q * per - start * lanes
            factors = turned[start - first][offset:offset + per, :]
            for i in range(per):
                factor = jnp.broadcast_to(factors[:, i:i + 1], (per, lanes))
                panels[q] = [
                    piece - factor * rows[i][start + b - first]
                    for b, piece in enumerate(panels[q])
                ]


def sketch_kernel(
    rows, slabs, pairs, points_ref, tests_ref, sketch_ref, core_ref, upper_ref,
    row_points, col_points, col_tests, part_out, part_in, plane, own_plane,
    gram_term, gram_in, gram_sum, core_term, core_in, core_sum,
    pt_sems, tt_sems, rp_sems, part_sems, plane_sems, term_sems, total_sems, own_sems,
):
    block = slabs * pairs
    me_row = lax.axis_index("row")
    me = lax.axis_index("slab") * pairs + lax.axis_index("pair")
    feats, width = points_ref.shape
    tests = tests_ref.shape[0]
    terms, term_in, total = (gram_term, core_term), (gram_in, core_in), (gram_sum, core_sum)
    mine = [
        pl.ds(pl.multiple_of(me * (term.shape[0] // block), term.shape[0] // block), term.shape[0] // block)
        for term in terms
    ]

    def at_row(d):
        return lax.rem(me_row + d, rows)

    def at_block(d):
        return lax.rem(me + d, block)

    def block_id(index):
        return {"slab": index // pairs, "pair": lax.rem(index, pairs)}

    def lanes(index):
        return pl.ds(pl.multiple_of(index * width, width), width)

    def copy(src, dst, sems, to, sender, target):
        return pltpu.make_async_remote_copy(
            src_ref=src, dst_ref=dst, send_sem=sems.at[0, to], recv_sem=sems.at[1, sender],
            device_id=target, device_id_type=MESH,
        )

    own_copies = [
        pltpu.make_async_copy(points_ref, row_points.at[me_row], own_sems.at[0]),
        pltpu.make_async_copy(points_ref, col_points.at[:, lanes(me)], own_sems.at[1]),
        pltpu.make_async_copy(tests_ref, col_tests.at[:, lanes(me)], own_sems.at[2]),
    ]
    barrier = pltpu.get_barrier_semaphore()
    loop(1, rows, lambda d: pl.semaphore_signal(
        barrier, inc=1, device_id={"row": at_row(d)}, device_id_type=MESH))
    loop(1, block, lambda d: pl.semaphore_signal(
        barrier, inc=1, device_id=block_id(at_block(d)), device_id_type=MESH))
    for own in own_copies:
        own.start()
    pl.semaphore_wait(barrier, rows + block - 2)

    def points_copy(to, sender):
        return copy(points_ref, col_points.at[:, lanes(sender)], pt_sems, to, sender, block_id(to))

    def tests_copy(to, sender):
        return copy(tests_ref, col_tests.at[:, lanes(sender)], tt_sems, to, sender, block_id(to))

    def row_copy(to, sender):
        return copy(points_ref, row_points.at[sender], rp_sems, to, sender, {"row": to})

    def part_copy(to, sender):
        return copy(part_out.at[to], part_in.at[sender], part_sems, to, sender, {"row": to})

    def plane_copy(to, sender):
        return copy(own_plane, plane.at[pl.ds(pl.multiple_of(sender * width, width), width), :],
                    plane_sems, to, sender, block_id(to))

    def term_copy(which, to, sender):
        return copy(terms[which].at[mine[which], :],
                    term_in[which].at[sender], term_sems.at[which], to, sender, {"row": to})

    def total_copy(which, to, sender):
        chunk = terms[which].shape[0] // block
        piece = pl.ds(pl.multiple_of(sender * chunk, chunk), chunk)
        return copy(total[which].at[piece, :], total[which].at[piece, :],
                    total_sems.at[which], to, sender, block_id(to))

    loop(1, block, lambda d: points_copy(at_block(d), me).start())
    loop(1, rows, lambda d: row_copy(at_row(d), me_row).start())
    loop(1, block, lambda d: tests_copy(at_block(d), me).start())
    for own in own_copies:
        own.wait()

    length_scale = 0.35 * math.sqrt(feats)
    scale = 5.0 / (length_scale * length_scale)
    loop(1, block, lambda d: points_copy(at_block(d), at_block(d)).wait_recv())
    cols = col_points[...]
    cols32 = cols.astype(jnp.float32)
    col_squares = jnp.sum(cols32 * cols32, axis=0, keepdims=True) * scale

    def partial_sketch(row):
        picked = row_points[row].astype(jnp.float32).T
        squares = jnp.sum(picked * picked, axis=1, keepdims=True) * scale
        inner = jnp.dot(picked.astype(jnp.bfloat16), cols, preferred_element_type=jnp.float32)
        squared = jnp.maximum(squares + col_squares - (2.0 * scale) * inner, 1e-30)
        t = squared * lax.rsqrt(squared)
        tile = ((1.0 + t + squared * (1.0 / 3.0)) * jnp.exp(-t)).astype(jnp.bfloat16)
        return lax.dot_general(tile, col_tests[...], (((1,), (1,)), ((), ())),
                               preferred_element_type=jnp.float32)

    loop(1, block, lambda d: tests_copy(at_block(d), at_block(d)).wait_recv())

    def row_step(d):
        to = at_row(d)
        row_copy(to, to).wait_recv()
        part_out[to] = partial_sketch(to).astype(jnp.bfloat16)
        part_copy(to, me_row).start()

    loop(1, rows, row_step)
    sketch_ref[...] = partial_sketch(me_row)

    def part_step(d):
        part_copy(at_row(d), at_row(d)).wait_recv()
        sketch_ref[...] += part_in[at_row(d)].astype(jnp.float32)

    loop(1, rows, part_step)

    rounded = sketch_ref[...].astype(jnp.bfloat16)
    own_plane[...] = rounded
    loop(1, block, lambda d: plane_copy(at_block(d), me).start())
    plane[pl.ds(pl.multiple_of(me * width, width), width), :] = rounded
    loop(1, block, lambda d: plane_copy(at_block(d), at_block(d)).wait_recv())
    whole = plane[...]
    lane = 128
    wide = tests // lane
    upper_blocks = [(a, b) for a in range(wide) for b in range(a, wide)]
    for place, (a, b) in enumerate(upper_blocks):
        gram_term[:, place * lane:(place + 1) * lane] = lax.dot_general(
            whole[:, a * lane:(a + 1) * lane], whole[:, b * lane:(b + 1) * lane],
            (((0,), (0,)), ((), ())), preferred_element_type=jnp.float32)
    loop(1, rows, lambda d: term_copy(0, at_row(d), me_row).start())
    core_term[...] = jnp.dot(col_tests[...], whole, preferred_element_type=jnp.float32)
    loop(1, rows, lambda d: term_copy(1, at_row(d), me_row).start())
    inverse = 1.0 / (width * rows * block)

    def sum_terms(which):
        term_in[which][me_row] = terms[which][mine[which], :]
        loop(1, rows, lambda d: term_copy(which, at_row(d), at_row(d)).wait_recv())
        total[which][mine[which], :] = jnp.sum(term_in[which][...], axis=0) * inverse
        loop(1, block, lambda d: total_copy(which, at_block(d), me).start())

    def take_total(which):
        loop(1, block, lambda d: total_copy(which, at_block(d), at_block(d)).wait_recv())

    sum_terms(0)
    take_total(0)
    blocks = {pair: gram_sum.at[:, place * lane:(place + 1) * lane]
              for place, pair in enumerate(upper_blocks)}
    factor(blocks, tests, upper_ref, lambda: sum_terms(1))
    take_total(1)
    core_ref[...] = core_sum[...]

    def block_sent(d):
        to = at_block(d)
        for sent in (points_copy, tests_copy, plane_copy):
            sent(to, me).wait_send()
        for which in (0, 1):
            total_copy(which, to, me).wait_send()

    def row_sent(d):
        to = at_row(d)
        row_copy(to, me_row).wait_send()
        part_copy(to, me_row).wait_send()
        for which in (0, 1):
            term_copy(which, to, me_row).wait_send()

    loop(1, block, block_sent)
    loop(1, rows, row_sent)


def local(sizes, points, test_matrix):
    rows, slabs, pairs = sizes
    block = slabs * pairs
    feats, width = points.shape
    tests = test_matrix.shape[0]
    vmem = pl.BlockSpec(memory_space=pltpu.VMEM)
    packed = tests * (tests // 128 + 1) // 2
    square = jax.ShapeDtypeStruct((tests, tests), jnp.float32)
    sketch, core_matrix, upper_factor = pl.pallas_call(
        functools.partial(sketch_kernel, rows, slabs, pairs),
        out_shape=(jax.ShapeDtypeStruct((width, tests), jnp.float32), square, square),
        in_specs=[pl.BlockSpec(memory_space=pl.ANY)] * 2,
        out_specs=(vmem, vmem, vmem),
        scratch_shapes=[
            pltpu.VMEM((rows, feats, width), jnp.bfloat16),
            pltpu.VMEM((feats, block * width), jnp.bfloat16),
            pltpu.VMEM((tests, block * width), jnp.bfloat16),
            pltpu.VMEM((rows, width, tests), jnp.bfloat16),
            pltpu.VMEM((rows, width, tests), jnp.bfloat16),
            pltpu.VMEM((block * width, tests), jnp.bfloat16),
            pltpu.VMEM((width, tests), jnp.bfloat16),
            pltpu.VMEM((128, packed), jnp.float32),
            pltpu.VMEM((rows, 128 // block, packed), jnp.float32),
            pltpu.VMEM((128, packed), jnp.float32),
            pltpu.VMEM((tests, tests), jnp.float32),
            pltpu.VMEM((rows, tests // block, tests), jnp.float32),
            pltpu.VMEM((tests, tests), jnp.float32),
            pltpu.SemaphoreType.DMA((2, block)),
            pltpu.SemaphoreType.DMA((2, block)),
            pltpu.SemaphoreType.DMA((2, rows)),
            pltpu.SemaphoreType.DMA((2, rows)),
            pltpu.SemaphoreType.DMA((2, block)),
            pltpu.SemaphoreType.DMA((2, 2, rows)),
            pltpu.SemaphoreType.DMA((2, 2, block)),
            pltpu.SemaphoreType.DMA((3,)),
        ],
        compiler_params=pltpu.CompilerParams(
            collective_id=0, has_side_effects=True, vmem_limit_bytes=60 * 1024 * 1024
        ),
        name="sketch",
    )(points, test_matrix)
    return (sketch, core_matrix, upper_factor)


def solution(mesh):
    sizes = tuple(mesh.shape[axis] for axis in ("row", "slab", "pair"))
    return jax.shard_map(
        functools.partial(local, sizes),
        mesh=mesh,
        in_specs=(P(None, ("job", "row", "slab", "pair")), P(None, ("row", "slab", "pair"))),
        out_specs=(P(("job", "row", "slab", "pair"), None), P("job", None), P("job", None)),
        check_vma=False,
    )
```

```python
import functools
import math

import jax
import jax.numpy as jnp
from jax import lax
from jax.experimental import pallas as pl
from jax.experimental.pallas import tpu as pltpu
from jax.sharding import PartitionSpec as P

MESH = pl.DeviceIdType.MESH


def loop(start, stop, body):
    if stop - start <= 8:
        for step in range(start, stop):
            body(step)
    else:
        lax.fori_loop(start, stop, lambda step, _: (body(step), 0)[1], 0)


def factor(blocks, size, upper_ref, halfway):
    per, lanes = 8, 128
    wide = size // lanes
    group = lanes // per
    panels = [
        [blocks[q // group, b][q % group * per:(q % group + 1) * per, :] for b in range(q // group, wide)]
        for q in range(size // per)
    ]
    row_id = lax.broadcasted_iota(jnp.int32, (per, lanes), 0)
    lane_id = lax.broadcasted_iota(jnp.int32, (per, lanes), 1)
    for p in range(size // per):
        if p == size // per // 2:
            halfway()
        first = p // group
        lane = p * per - first * lanes
        panel = panels[p]
        columns = [jnp.broadcast_to(panel[0][:, lane + j:lane + j + 1], (per, lanes)) for j in range(per)]
        small = [[columns[j][i:i + 1, :] for j in range(per)] for i in range(per)]
        rows = [[piece[i:i + 1, :] for piece in panel] for i in range(per)]
        for i in range(per):
            inverse = lax.rsqrt(small[i][i])
            for j in range(i + 1, per):
                small[i][j] = small[i][j] * inverse
            rows[i] = [piece * inverse for piece in rows[i]]
            for j in range(i + 1, per):
                for l in range(j, per):
                    small[j][l] = small[j][l] - small[i][j] * small[i][l]
                rows[j] = [a - small[i][j] * b for a, b in zip(rows[j], rows[i])]
        done = [jnp.concatenate([rows[i][b] for i in range(per)], axis=0) for b in range(wide - first)]
        done[0] = jnp.where(lane_id >= row_id + lane, done[0], 0.0)
        for b in range(wide):
            upper_ref[p * per:(p + 1) * per, b * lanes:(b + 1) * lanes] = (
                done[b - first] if b >= first else jnp.zeros((per, lanes), jnp.float32))
        turned = [piece.T for piece in done]
        for q in range(p + 1, size // per):
            start = q // group
            offset = q * per - start * lanes
            factors = turned[start - first][offset:offset + per, :]
            for i in range(per):
                factor = jnp.broadcast_to(factors[:, i:i + 1], (per, lanes))
                panels[q] = [
                    piece - factor * rows[i][start + b - first]
                    for b, piece in enumerate(panels[q])
                ]


def sketch_kernel(
    rows, slabs, pairs, points_ref, tests_ref, sketch_ref, core_ref, upper_ref,
    row_points, col_points, col_tests, tiles, part_out, part_in, plane, own_plane,
    gram_term, gram_in, gram_sum, core_term, core_in, core_sum,
    pt_sems, tt_sems, rp_sems, part_sems, plane_sems, term_sems, total_sems, own_sems,
):
    block = slabs * pairs
    me_row = lax.axis_index("row")
    me = lax.axis_index("slab") * pairs + lax.axis_index("pair")
    feats, width = points_ref.shape
    tests = tests_ref.shape[0]
    terms, term_in, total = (gram_term, core_term), (gram_in, core_in), (gram_sum, core_sum)
    mine = [
        pl.ds(pl.multiple_of(me * (term.shape[0] // block), term.shape[0] // block), term.shape[0] // block)
        for term in terms
    ]

    def at_row(d):
        return lax.rem(me_row + d, rows)

    def at_block(d):
        return lax.rem(me + d, block)

    def block_id(index):
        return {"slab": index // pairs, "pair": lax.rem(index, pairs)}

    def lanes(index):
        return pl.ds(pl.multiple_of(index * width, width), width)

    def copy(src, dst, sems, to, sender, target):
        return pltpu.make_async_remote_copy(
            src_ref=src, dst_ref=dst, send_sem=sems.at[0, to], recv_sem=sems.at[1, sender],
            device_id=target, device_id_type=MESH,
        )

    own_copies = [
        pltpu.make_async_copy(points_ref, row_points.at[me_row], own_sems.at[0]),
        pltpu.make_async_copy(points_ref, col_points.at[:, lanes(me)], own_sems.at[1]),
        pltpu.make_async_copy(tests_ref, col_tests.at[:, lanes(me)], own_sems.at[2]),
    ]
    barrier = pltpu.get_barrier_semaphore()
    loop(1, rows, lambda d: pl.semaphore_signal(
        barrier, inc=1, device_id={"row": at_row(d)}, device_id_type=MESH))
    loop(1, block, lambda d: pl.semaphore_signal(
        barrier, inc=1, device_id=block_id(at_block(d)), device_id_type=MESH))
    for own in own_copies:
        own.start()
    pl.semaphore_wait(barrier, rows + block - 2)

    def points_copy(to, sender):
        return copy(points_ref, col_points.at[:, lanes(sender)], pt_sems, to, sender, block_id(to))

    def tests_copy(to, sender):
        return copy(tests_ref, col_tests.at[:, lanes(sender)], tt_sems, to, sender, block_id(to))

    def row_copy(to, sender):
        return copy(points_ref, row_points.at[sender], rp_sems, to, sender, {"row": to})

    def part_copy(to, sender):
        return copy(part_out.at[to], part_in.at[sender], part_sems, to, sender, {"row": to})

    def plane_copy(to, sender):
        return copy(own_plane, plane.at[pl.ds(pl.multiple_of(sender * width, width), width), :],
                    plane_sems, to, sender, block_id(to))

    def term_copy(which, to, sender):
        return copy(terms[which].at[mine[which], :],
                    term_in[which].at[sender], term_sems.at[which], to, sender, {"row": to})

    def total_copy(which, to, sender):
        chunk = terms[which].shape[0] // block
        piece = pl.ds(pl.multiple_of(sender * chunk, chunk), chunk)
        return copy(total[which].at[piece, :], total[which].at[piece, :],
                    total_sems.at[which], to, sender, block_id(to))

    loop(1, block, lambda d: points_copy(at_block(d), me).start())
    loop(1, rows, lambda d: row_copy(at_row(d), me_row).start())
    loop(1, block, lambda d: tests_copy(at_block(d), me).start())
    for own in own_copies:
        own.wait()

    length_scale = 0.35 * math.sqrt(feats)
    scale = 5.0 / (length_scale * length_scale)
    loop(1, block, lambda d: points_copy(at_block(d), at_block(d)).wait_recv())
    cols = col_points[...]
    cols32 = cols.astype(jnp.float32)
    col_squares = jnp.sum(cols32 * cols32, axis=0, keepdims=True) * scale

    def make_tile(row):
        picked = row_points[row].astype(jnp.float32).T
        squares = jnp.sum(picked * picked, axis=1, keepdims=True) * scale
        inner = jnp.dot(picked.astype(jnp.bfloat16), cols, preferred_element_type=jnp.float32)
        squared = jnp.maximum(squares + col_squares - (2.0 * scale) * inner, 1e-30)
        t = squared * lax.rsqrt(squared)
        tiles[row] = ((1.0 + t + squared * (1.0 / 3.0)) * jnp.exp(-t)).astype(jnp.bfloat16)

    def partial_sketch(row):
        return lax.dot_general(tiles[row], col_tests[...], (((1,), (1,)), ((), ())),
                               preferred_element_type=jnp.float32)

    def tile_step(d):
        row_copy(at_row(d), at_row(d)).wait_recv()
        make_tile(at_row(d))

    make_tile(me_row)
    loop(1, rows, tile_step)
    loop(1, block, lambda d: tests_copy(at_block(d), at_block(d)).wait_recv())

    def row_step(d):
        to = at_row(d)
        part_out[to] = partial_sketch(to).astype(jnp.bfloat16)
        part_copy(to, me_row).start()

    loop(1, rows, row_step)
    sketch_ref[...] = partial_sketch(me_row)

    def part_step(d):
        part_copy(at_row(d), at_row(d)).wait_recv()
        sketch_ref[...] += part_in[at_row(d)].astype(jnp.float32)

    loop(1, rows, part_step)

    rounded = sketch_ref[...].astype(jnp.bfloat16)
    own_plane[...] = rounded
    loop(1, block, lambda d: plane_copy(at_block(d), me).start())
    plane[pl.ds(pl.multiple_of(me * width, width), width), :] = rounded
    loop(1, block, lambda d: plane_copy(at_block(d), at_block(d)).wait_recv())
    whole = plane[...]
    lane = 128
    wide = tests // lane
    upper_blocks = [(a, b) for a in range(wide) for b in range(a, wide)]
    for place, (a, b) in enumerate(upper_blocks):
        gram_term[:, place * lane:(place + 1) * lane] = lax.dot_general(
            whole[:, a * lane:(a + 1) * lane], whole[:, b * lane:(b + 1) * lane],
            (((0,), (0,)), ((), ())), preferred_element_type=jnp.float32)
    loop(1, rows, lambda d: term_copy(0, at_row(d), me_row).start())
    core_term[...] = jnp.dot(col_tests[...], whole, preferred_element_type=jnp.float32)
    inverse = 1.0 / (width * rows * block)

    def sum_terms(which):
        term_in[which][me_row] = terms[which][mine[which], :]
        loop(1, rows, lambda d: term_copy(which, at_row(d), at_row(d)).wait_recv())
        total[which][mine[which], :] = jnp.sum(term_in[which][...], axis=0) * inverse
        loop(1, block, lambda d: total_copy(which, at_block(d), me).start())

    def take_total(which):
        loop(1, block, lambda d: total_copy(which, at_block(d), at_block(d)).wait_recv())

    sum_terms(0)
    loop(1, rows, lambda d: term_copy(1, at_row(d), me_row).start())
    take_total(0)
    blocks = {pair: gram_sum.at[:, place * lane:(place + 1) * lane]
              for place, pair in enumerate(upper_blocks)}
    factor(blocks, tests, upper_ref, lambda: sum_terms(1))
    take_total(1)
    core_ref[...] = core_sum[...]

    def block_sent(d):
        to = at_block(d)
        for sent in (points_copy, tests_copy, plane_copy):
            sent(to, me).wait_send()
        for which in (0, 1):
            total_copy(which, to, me).wait_send()

    def row_sent(d):
        to = at_row(d)
        row_copy(to, me_row).wait_send()
        part_copy(to, me_row).wait_send()
        for which in (0, 1):
            term_copy(which, to, me_row).wait_send()

    loop(1, block, block_sent)
    loop(1, rows, row_sent)


def write_out(sketch_ref, core_ref, upper_ref, sketch_out, core_out, upper_out, sems):
    copies = [
        pltpu.make_async_copy(source, target, sems.at[place])
        for place, (source, target) in enumerate(
            ((sketch_ref, sketch_out), (core_ref, core_out), (upper_ref, upper_out)))
    ]
    for one in copies:
        one.start()
    for one in copies:
        one.wait()


def local(sizes, points, test_matrix):
    rows, slabs, pairs = sizes
    block = slabs * pairs
    feats, width = points.shape
    tests = test_matrix.shape[0]
    vmem = pl.BlockSpec(memory_space=pltpu.VMEM)
    hbm = pl.BlockSpec(memory_space=pl.ANY)
    packed = tests * (tests // 128 + 1) // 2
    square = jax.ShapeDtypeStruct((tests, tests), jnp.float32)
    shapes = (jax.ShapeDtypeStruct((width, tests), jnp.float32), square, square)
    results = pl.pallas_call(
        functools.partial(sketch_kernel, rows, slabs, pairs),
        out_shape=shapes,
        in_specs=[hbm, hbm],
        out_specs=(vmem, vmem, vmem),
        scratch_shapes=[
            pltpu.VMEM((rows, feats, width), jnp.bfloat16),
            pltpu.VMEM((feats, block * width), jnp.bfloat16),
            pltpu.VMEM((tests, block * width), jnp.bfloat16),
            pltpu.VMEM((rows, width, block * width), jnp.bfloat16),
            pltpu.VMEM((rows, width, tests), jnp.bfloat16),
            pltpu.VMEM((rows, width, tests), jnp.bfloat16),
            pltpu.VMEM((block * width, tests), jnp.bfloat16),
            pltpu.VMEM((width, tests), jnp.bfloat16),
            pltpu.VMEM((128, packed), jnp.float32),
            pltpu.VMEM((rows, 128 // block, packed), jnp.float32),
            pltpu.VMEM((128, packed), jnp.float32),
            pltpu.VMEM((tests, tests), jnp.float32),
            pltpu.VMEM((rows, tests // block, tests), jnp.float32),
            pltpu.VMEM((tests, tests), jnp.float32),
            pltpu.SemaphoreType.DMA((2, block)),
            pltpu.SemaphoreType.DMA((2, block)),
            pltpu.SemaphoreType.DMA((2, rows)),
            pltpu.SemaphoreType.DMA((2, rows)),
            pltpu.SemaphoreType.DMA((2, block)),
            pltpu.SemaphoreType.DMA((2, 2, rows)),
            pltpu.SemaphoreType.DMA((2, 2, block)),
            pltpu.SemaphoreType.DMA((3,)),
        ],
        compiler_params=pltpu.CompilerParams(
            collective_id=0, has_side_effects=True, vmem_limit_bytes=60 * 1024 * 1024
        ),
        name="sketch",
    )(points, test_matrix)
    return pl.pallas_call(
        write_out,
        out_shape=shapes,
        in_specs=[hbm] * 3,
        out_specs=(hbm, hbm, hbm),
        scratch_shapes=[pltpu.SemaphoreType.DMA((3,))],
        name="write_out",
    )(*results)


def solution(mesh):
    sizes = tuple(mesh.shape[axis] for axis in ("row", "slab", "pair"))
    return jax.shard_map(
        functools.partial(local, sizes),
        mesh=mesh,
        in_specs=(P(None, ("job", "row", "slab", "pair")), P(None, ("row", "slab", "pair"))),
        out_specs=(P(("job", "row", "slab", "pair"), None), P("job", None), P("job", None)),
        check_vma=False,
    )
```
